128 devices in a mesh: col: 8 (over y_hi, x), ex: 16 (over z, y_lo, core).
Axes of the slice: x: 4, y: 4 (y_hi: 2, y_lo: 2; y = y_hi * 2 + y_lo), z: 4, core: 2. Of those that a mesh axis runs over, the one named last changes fastest.
Arguments:
- features: bfloat16 [8192, 8192], P('ex', 'col'), as said below
Outputs:
- gram: float32 [8192, 8192], P(('col', 'ex'))
Inputs may be any that keep to these rules, and one draw needn't show every extreme that they name: `features`: Real-valued projected gradients.
All inputs are finite; a program needn't handle non-finite values.
Results may differ from the reference program's by a relative error of at most 0.0003.
Values may be sent and summed in bfloat16 or wider, within the bound.
No kernel may reach another device: no remote copies, remote signals or barrier semaphores. Data moves between devices by JAX's collectives and lax.ppermute only.
A program may use at most 192 MiB of HBM per device.

```python
import math
import jax
import jax.numpy as jnp

K = 8192
SLAB = 8192


def draw_features(key, part):
    key = jax.random.fold_in(key, 11)
    keys = jax.random.split(key, 5)
    noise = jax.random.normal(keys[0], (SLAB, K), jnp.float32)
    common = jax.random.normal(keys[1], (SLAB, 1), jnp.float32)
    row_scale = jnp.exp(jax.random.uniform(keys[2], (SLAB, 1), jnp.float32, 0.0, math.log(10.0)))
    col_scale = jnp.exp(jax.random.uniform(keys[3], (1, K), jnp.float32, 0.0, math.log(4.0)))
    direction = jax.random.normal(keys[4], (1, K), jnp.float32)
    values = row_scale * (noise * col_scale + 0.7 * common * direction)
    values = values / (4.6 * math.sqrt(SLAB))
    return values.astype(jnp.bfloat16)


def setup_inputs(seed: int = 0) -> dict:
    key_list = jax.random.split(jax.random.key(seed), 2)
    return {
        "features": draw_features(jax.random.fold_in(key_list[1], 71), 0),
    }


damping = 0.5


def reference(features):
    cross = jnp.dot(features.T, features, preferred_element_type=jnp.float32)
    diag_index = jnp.arange(K, dtype=jnp.int32)
    return cross.at[diag_index, diag_index].add(jnp.float32(damping))
```

```python
import jax
import jax.numpy as jnp
from jax import lax
from jax.sharding import Mesh, PartitionSpec as P

damping = 0.5
parts = ("yh", "x", "z", "yl", "core")
sizes = (2, 4, 4, 2, 2)
ring = ("yh", "yl")


def swap(value, axis):
    return lax.ppermute(value, axis, [(0, 1), (1, 0)])


def trade(value, axis, bits):
    return lax.ppermute(value, axis, [(i, i ^ bits) for i in range(4)])


def ring_gather(value, axis):
    near = trade(value, axis, 1)
    far = trade(value, axis, 3)
    half = value.shape[0] // 2
    opposite = jnp.concatenate([trade(far[:half], axis, 1), trade(near[half:], axis, 3)], 0)
    return value, near, opposite, far


def pick(value, index, axis):
    return lax.dynamic_index_in_dim(value, index, axis, keepdims=False)


def add_damping(result):
    strip = result.shape[0]
    owner = jnp.int32(0)
    for name, size in zip(parts, sizes):
        owner = owner * size + lax.axis_index(name)
    row_ids = owner * strip + lax.broadcasted_iota(jnp.int32, result.shape, 0)
    col_ids = lax.broadcasted_iota(jnp.int32, result.shape, 1)
    return result + jnp.where(row_ids == col_ids, jnp.float32(damping), jnp.float32(0.0))


def per_device(features):
    yh, x, yl, core = (lax.axis_index(name) for name in ("yh", "x", "yl", "core"))
    rows, cols = features.shape
    strip = cols // 8

    largest = lax.pmax(jnp.max(jnp.abs(features)).astype(jnp.float32), parts)
    largest = jnp.maximum(largest, jnp.float32(1e-18))
    shrink, grow = 4.0 / largest, largest * 0.25

    split = features.reshape(rows, 4, 2, strip)
    kept = pick(split, yl, 2).reshape(rows, cols // 2)
    given = pick(split, 1 - yl, 2).reshape(rows, cols // 2)
    left = ring_gather(jnp.concatenate([kept, swap(given, "yl")], 0), "x")
    left = jnp.concatenate(left, 1)
    left = jnp.concatenate([left, swap(left, "core")], 0)

    own, near, opposite, far = ring_gather(features, ring)
    right = jnp.concatenate([jnp.concatenate([own, near], 0), jnp.concatenate([opposite, far], 0)], 1)
    right = right.reshape(2 * rows, 2, 2, cols // 2)
    kept = pick(right, core, 2).reshape(2 * rows, cols)
    given = pick(right, 1 - core, 2).reshape(2 * rows, cols)
    right = jnp.concatenate([kept, swap(given, "core")], 0)

    tile = lax.dot_general(left, right, (((0,), (0,)), ((), ())), preferred_element_type=jnp.float32)
    tile = (tile * shrink * shrink).astype(jnp.float16).reshape(4, 4, strip, cols)
    packed = jnp.stack([pick(tile, x ^ n, 0) for n in range(4)]).reshape(16, strip, cols)
    came = lax.all_to_all(packed, ("x", "z"), 0, 0, tiled=True)
    came = came.reshape(4, 4, strip, cols).astype(jnp.float32).sum(1) * grow * grow

    came = came.reshape(4, 2, strip // 2, 2, cols // 2)
    kept = pick(came, core, 1)
    got = swap(pick(came, 1 - core, 1), "core")
    low, high = jnp.where(core == 0, kept, got), jnp.where(core == 0, got, kept)
    both = jnp.stack([low, high], 3)
    both = jnp.where(yh == 0, both, both[:, :, ::-1])
    result = both.transpose(1, 2, 0, 3, 4).reshape(strip // 2, 8 * cols)
    return add_damping(result)


def solution(mesh):
    fine = Mesh(mesh.devices.reshape(sizes), parts)
    return jax.shard_map(
        per_device,
        mesh=fine,
        in_specs=(P(("z", "yl", "core"), ("yh", "x")),),
        out_specs=P(parts, None),
        check_vma=False,
    )
```

```python
import jax
import jax.numpy as jnp
from jax import lax
from jax.experimental import pallas as pl
from jax.experimental.pallas import tpu as pltpu
from jax.sharding import Mesh, PartitionSpec as P

damping = 0.5
parts = ("yh", "x", "z", "yl", "core")
sizes = (2, 4, 4, 2, 2)
ring = ("yh", "yl")
mib = 1024 * 1024
lane = 128
top_power = 14.0


def swap(value):
    return lax.ppermute(value, "core", [(0, 1), (1, 0)])


def trade(value, axis, bits):
    return lax.ppermute(value, axis, [(i, i ^ bits) for i in range(4)])


def after(value, *others):
    return lax.optimization_barrier((value, *others))[0]


vmem = pl.BlockSpec(memory_space=pltpu.VMEM)
smem = pl.BlockSpec(memory_space=pltpu.SMEM)


def split_kernel(place, block, theirs, both):
    yl = place[0]
    for slab in range(4):
        here = slice(slab * lane, (slab + 1) * lane)
        for other in range(2):
            start = pl.multiple_of((slab * 2 + (yl ^ other)) * lane, lane)
            some = block[:, pl.ds(start, lane)]
            both[other, :, here] = some
            if other:
                theirs[:, here] = some


def split(features, yl):
    rows, cols = features.shape
    return pl.pallas_call(
        split_kernel,
        in_specs=[smem, vmem],
        out_specs=[vmem] * 2,
        out_shape=[
            jax.ShapeDtypeStruct((rows, cols // 2), features.dtype),
            jax.ShapeDtypeStruct((2, rows, cols // 2), features.dtype),
        ],
        compiler_params=pltpu.CompilerParams(vmem_limit_bytes=16 * mib),
    )(jnp.stack([yl]), features)


def turn_kernel(place, *refs):
    core = place[0]
    *blocks, out = refs
    part = lane // 2
    for which, block in enumerate(blocks):
        for slab in range(4):
            here = slice(slab * lane, (slab + 1) * lane)
            turned = (block[0, :, here] if len(block.shape) == 3 else block[:, here]).T
            out[which, slab * part : (slab + 1) * part, :] = jnp.where(core == 0, turned[:part], turned[part:])


def turn(block, away, core):
    rows, cols = block.shape[-2:]
    return pl.pallas_call(
        turn_kernel,
        in_specs=[smem, vmem, vmem],
        out_specs=vmem,
        out_shape=jax.ShapeDtypeStruct((2, cols // 2, rows), block.dtype),
        compiler_params=pltpu.CompilerParams(vmem_limit_bytes=16 * mib),
    )(jnp.stack([core]), block, away)


def weights(cols):
    return 1.0 + lax.broadcasted_iota(jnp.int32, (1, cols), 1).astype(jnp.float32) / cols


def product(ns, x, lefts, rights, result=None):
    flat = [part for n in ns for part in lefts[n]]
    arrays, picks = zip(*rights)
    rows, depth, cols, block = flat[0].shape[1], flat[0].shape[2], arrays[0].shape[-1], 256
    part, one = rows // 4, result is not None

    def kernel(where, *refs):
        out = refs[-1]
        col = pl.program_id(0) * block + lax.broadcasted_iota(jnp.int32, (1, block), 1)
        weight = 1.0 + col.astype(jnp.float32) / cols
        for i, n in enumerate(ns):
            at = 0 if one else where[0] ^ n
            kept, got = refs[2 * i], refs[2 * i + 1]
            terms = (kept[0], kept[1], got[0], got[1])
            for c in range(2):
                total = None
                for t, left in enumerate(terms):
                    right = refs[len(flat) + 4 * c + t]
                    right = right[0] if len(right.shape) == 3 else right[...]
                    term = jnp.dot(left, right, preferred_element_type=jnp.float32)
                    total = term if total is None else total + term
                most = jnp.max(jnp.max(jnp.abs(total), axis=0, keepdims=True), axis=1, keepdims=True)
                power = jnp.ceil(jnp.log2(jnp.maximum(most, jnp.float32(1e-30)))) - top_power
                total = total * (jnp.exp2(-power) * weight)
                power = jnp.broadcast_to(power, (4, block))
                for slab in range(4):
                    out[at, slab, c * part : (c + 1) * part, :] = total[slab * part : (slab + 1) * part]
                    out[at, slab, 2 * part + 4 * c : 2 * part + 4 * c + 4, :] = power

    specs = [pl.BlockSpec(v.shape, lambda i, where: (0, 0, 0)) for v in flat]
    for pick in picks:
        if pick is None:
            specs.append(pl.BlockSpec((depth, block), lambda i, where: (0, i)))
        else:
            specs.append(pl.BlockSpec((1, depth, block), lambda i, where, pick=pick: (pick, 0, i)))
    height = 2 * part + 8
    if one:
        specs.append(pl.BlockSpec(memory_space=pl.ANY))
        out_spec = pl.BlockSpec((1, 4, height, block), lambda i, where: (where[0] ^ ns[0], 0, 0, i))
    else:
        out_spec = pl.BlockSpec((4, 4, height, block), lambda i, where: (0, 0, 0, i))
    return pl.pallas_call(
        kernel,
        grid_spec=pltpu.PrefetchScalarGridSpec(
            num_scalar_prefetch=1, grid=(cols // block,), in_specs=specs, out_specs=out_spec
        ),
        out_shape=jax.ShapeDtypeStruct((4, 4, height, cols), jnp.float32),
        input_output_aliases={len(specs): 0} if one else {},
        compiler_params=pltpu.CompilerParams(vmem_limit_bytes=32 * mib),
        cost_estimate=pl.CostEstimate(
            flops=2 * rows * cols * depth * len(arrays) * len(ns), bytes_accessed=8 * mib, transcendentals=0
        ),
    )(jnp.stack([x]), *flat, *arrays, *([result] if one else []))


def place_kernel(where, sums, *refs):
    out = refs[-1]
    first_row, yl = where[1], where[2]
    rows, width = sums.shape[2], 2 * sums.shape[3]
    for i in range(4):
        row_ids = first_row + lax.broadcasted_iota(jnp.int32, (rows, width), 0)
        col_ids = (where[0] * 4 + i) * width + lax.broadcasted_iota(jnp.int32, (rows, width), 1)
        damp = jnp.where(row_ids == col_ids, jnp.float32(damping), jnp.float32(0.0))
        for slab in range(4):
            here = slice(slab * lane, (slab + 1) * lane)
            mine, theirs = sums[i, 0, :, here], sums[i, 1, :, here]
            for other in range(2):
                at = (2 * slab + other) * lane
                there = slice(i * width + at, i * width + at + lane)
                out[:, there] = jnp.where(yl == other, mine, theirs) + damp[:, at : at + lane]


def place(sums, where, result):
    rows, width = sums.shape[2], 8 * sums.shape[3]
    given = [] if result is None else [result]
    return pl.pallas_call(
        place_kernel,
        grid_spec=pltpu.PrefetchScalarGridSpec(
            num_scalar_prefetch=1,
            grid=(1,),
            in_specs=[pl.BlockSpec(sums.shape, lambda i, where: (0, 0, 0, 0))]
            + [pl.BlockSpec(memory_space=pl.ANY)] * len(given),
            out_specs=pl.BlockSpec((rows, width), lambda i, where: (0, where[0])),
        ),
        out_shape=jax.ShapeDtypeStruct((rows, 2 * width), jnp.float32),
        input_output_aliases={2: 0} if given else {},
        compiler_params=pltpu.CompilerParams(vmem_limit_bytes=16 * mib),
    )(where, sums, *given)


def per_device(features):
    yh, x, z, yl, core = (lax.axis_index(name) for name in parts)
    rows, cols = features.shape
    half, part = cols // 2, cols // 16

    theirs, both = split(features, yl)
    near_mine = trade(theirs, ring, 1)
    both_away = swap(both)
    kept = turn(both[:1], both_away[:1], core)
    kept_near, kept_far = trade(kept, "x", 1), trade(kept, "x", 3)
    near_mine_away = swap(after(near_mine, kept_near, kept_far))
    near_theirs = trade(after(both[0], near_mine), ring, 1)
    far = trade(both, ring, 3)
    got = turn(near_mine[None], near_mine_away[None], core)
    got_near, got_far = trade(got, "x", 1), trade(got, "x", 3)
    kept_opposite = trade(after(kept_far, got_near), "x", 1)
    got_opposite = trade(got_near, "x", 3)
    lefts = [(kept, got), (kept_near, got_near), (kept_opposite, got_opposite), (kept_far, got_far)]
    near_theirs_away = swap(after(near_theirs, got_near, got_far))

    first = [(both, 0), (both_away, 0), (near_mine, None), (near_mine_away, None)]
    first += [(both, 1), (both_away, 1), (near_theirs, None), (near_theirs_away, None)]
    tile = product([0, 1, 3], x, lefts, first)
    tile = product([2], x, lefts, first, tile)

    opposite_mine = trade(after(far[0], got_near, got_far), ring, 1)
    opposite_theirs = trade(after(near_mine, got_near, got_far), ring, 3)
    far_away = swap(after(far, got_near, got_far))
    second = [(opposite_mine, None), (swap(opposite_mine), None), (far, 1), (far_away, 1)]
    second += [(opposite_theirs, None), (swap(opposite_theirs), None), (far, 0), (far_away, 0)]

    first_row = ((((yh * 4 + x) * 4 + z) * 2 + yl) * 2 + core) * part
    result = None
    for side in range(2):
        if side:
            tile = product([0, 1, 2, 3], x, lefts, second)
        packed = tile.astype(jnp.float16).reshape(16, 2 * part + 8, half)
        came = lax.all_to_all(packed, ("x", "z"), 0, 0, tiled=True)
        if side:
            came = after(came, result)
        came = came.reshape(4, 4, 2 * part + 8, half)
        power = came[:, :, 2 * part :: 4].astype(jnp.float32)
        grow = jnp.exp2(power) / weights(half)
        sums = came[:, :, : 2 * part].astype(jnp.float32).reshape(4, 4, 2, part, half) * grow[:, :, :, None]
        sums = sums.sum(1)
        result = place(sums, jnp.stack([yh ^ side, first_row, yl]), result)
    return result


def solution(mesh):
    fine = Mesh(mesh.devices.reshape(sizes), parts)
    return jax.shard_map(
        per_device,
        mesh=fine,
        in_specs=(P(("z", "yl", "core"), ("yh", "x")),),
        out_specs=P(parts, None),
        check_vma=False,
    )
```

```python
import jax
import jax.numpy as jnp
from jax import lax
from jax.experimental import pallas as pl
from jax.experimental.pallas import tpu as pltpu
from jax.sharding import Mesh, PartitionSpec as P

damping = 0.5
parts = ("yh", "x", "z", "yl", "core")
sizes = (2, 4, 4, 2, 2)
ring = ("yh", "yl")
mib = 1024 * 1024
lane = 128
top_power = 14.0


def swap(value):
    return lax.ppermute(value, "core", [(0, 1), (1, 0)])


def trade(value, axis, bits):
    return lax.ppermute(value, axis, [(i, i ^ bits) for i in range(4)])


def together(*values):
    return lax.optimization_barrier(values)


def after(value, *others):
    return lax.optimization_barrier((value, *others))[0]


vmem = pl.BlockSpec(memory_space=pltpu.VMEM)
smem = pl.BlockSpec(memory_space=pltpu.SMEM)


def split_kernel(place, block, theirs, both):
    yl = place[0]
    for slab in range(4):
        here = slice(slab * lane, (slab + 1) * lane)
        for other in range(2):
            start = pl.multiple_of((slab * 2 + (yl ^ other)) * lane, lane)
            some = block[:, pl.ds(start, lane)]
            both[other, :, here] = some
            if other:
                theirs[:, here] = some


def split(features, yl):
    rows, cols = features.shape
    return pl.pallas_call(
        split_kernel,
        in_specs=[smem, vmem],
        out_specs=[vmem] * 2,
        out_shape=[
            jax.ShapeDtypeStruct((rows, cols // 2), features.dtype),
            jax.ShapeDtypeStruct((2, rows, cols // 2), features.dtype),
        ],
        compiler_params=pltpu.CompilerParams(vmem_limit_bytes=16 * mib),
    )(jnp.stack([yl]), features)


def turn_kernel(place, *refs):
    core = place[0]
    *blocks, out = refs
    part = lane // 2
    for which, block in enumerate(blocks):
        for slab in range(4):
            here = slice(slab * lane, (slab + 1) * lane)
            turned = (block[0, :, here] if len(block.shape) == 3 else block[:, here]).T
            out[which, slab * part : (slab + 1) * part, :] = jnp.where(core == 0, turned[:part], turned[part:])


def turn(block, away, core):
    rows, cols = block.shape[-2:]
    first = pl.BlockSpec((1, rows, cols), lambda i: (0, 0, 0)) if block.ndim == 3 else pl.BlockSpec((rows, cols), lambda i: (0, 0))
    return pl.pallas_call(
        turn_kernel,
        grid=(1,),
        in_specs=[smem, first, first],
        out_specs=pl.BlockSpec((2, cols // 2, rows), lambda i: (0, 0, 0)),
        out_shape=jax.ShapeDtypeStruct((2, cols // 2, rows), block.dtype),
        compiler_params=pltpu.CompilerParams(vmem_limit_bytes=16 * mib),
    )(jnp.stack([core]), block, away)


def weights(cols):
    return 1.0 + lax.broadcasted_iota(jnp.int32, (1, cols), 1).astype(jnp.float32) / cols


def product(ns, turn_by, lefts, rights, by_z=False, result=None):
    flat = [part for n in ns for part in lefts[n]]
    starts = [sum(len(lefts[m]) for m in ns[:i]) for i in range(len(ns))]
    arrays, picks = zip(*rights)
    rows, depth, cols, block = flat[0].shape[-2], flat[0].shape[-1], arrays[0].shape[-1], 256
    eights, one = rows // 4 // 8, result is not None

    def kernel(where, *refs):
        out = refs[-1]
        col = pl.program_id(0) * block + lax.broadcasted_iota(jnp.int32, (1, block), 1)
        weight = 1.0 + col.astype(jnp.float32) / cols
        for i, n in enumerate(ns):
            terms = []
            for ref in refs[starts[i] : starts[i] + len(lefts[n])]:
                terms += [ref[0], ref[1]] if len(ref.shape) == 3 else [ref[...]]
            totals, most = [], jnp.full((1, 1), 1e-30, jnp.float32)
            for c in range(2):
                total = None
                for t, left in enumerate(terms):
                    right = refs[len(flat) + 4 * c + t]
                    right = right[0] if len(right.shape) == 3 else right[...]
                    term = jnp.dot(left, right, preferred_element_type=jnp.float32)
                    total = term if total is None else total + term
                totals.append(total)
                most = jnp.maximum(most, jnp.max(jnp.max(jnp.abs(total), axis=0, keepdims=True), axis=1, keepdims=True))
            power = jnp.ceil(jnp.log2(most)) - top_power
            shrink = jnp.exp2(-power) * weight
            for slab in range(4):
                if by_z:
                    at = (slab ^ where[0], i)
                else:
                    at = (0 if one else where[0] ^ n, slab)
                for c in range(2):
                    some = totals[c][slab * 8 * eights : (slab + 1) * 8 * eights] * shrink
                    out[(*at, slice(c * eights, (c + 1) * eights))] = some.reshape(eights, 8, block)
                out[(*at, 2 * eights)] = jnp.broadcast_to(power, (8, block))

    specs = [pl.BlockSpec(v.shape, lambda i, where, dims=v.ndim: (0,) * dims) for v in flat]
    for pick in picks:
        if pick is None:
            specs.append(pl.BlockSpec((depth, block), lambda i, where: (0, i)))
        else:
            specs.append(pl.BlockSpec((1, depth, block), lambda i, where, pick=pick: (pick, 0, i)))
    height = 2 * eights + 1
    if one:
        specs.append(pl.BlockSpec(memory_space=pl.ANY))
    count = len(ns) if by_z else 4
    if one:
        out_spec = pl.BlockSpec((1, 4, height, 8, block), lambda i, where: (where[0] ^ ns[0], 0, 0, 0, i))
    else:
        out_spec = pl.BlockSpec((4, count, height, 8, block), lambda i, where: (0, 0, 0, 0, i))
    return pl.pallas_call(
        kernel,
        grid_spec=pltpu.PrefetchScalarGridSpec(
            num_scalar_prefetch=1, grid=(cols // block,), in_specs=specs, out_specs=out_spec
        ),
        out_shape=jax.ShapeDtypeStruct((4, count, height, 8, cols), jnp.float32),
        input_output_aliases={len(specs): 0} if one else {},
        compiler_params=pltpu.CompilerParams(vmem_limit_bytes=32 * mib),
        cost_estimate=pl.CostEstimate(
            flops=2 * rows * cols * depth * len(arrays) * len(ns), bytes_accessed=8 * mib, transcendentals=0
        ),
    )(jnp.stack([turn_by]), *flat, *arrays, *([result] if one else []))


def unscale(value):
    grow = jnp.exp2(value[..., -1:, :, :].astype(jnp.float32)) / weights(value.shape[-1])
    return value[..., :-1, :, :].astype(jnp.float32) * grow


def place(sums, where, result=None):
    _, rows, half = sums[0].shape
    width = 2 * half
    given = [] if result is None else [result]

    def kernel(where, *refs):
        out = refs[-1]
        for i in range(4):
            block = where[3 + i]
            row_ids = where[1] + lax.broadcasted_iota(jnp.int32, (rows, width), 0)
            col_ids = (where[0] * 4 + block) * width + lax.broadcasted_iota(jnp.int32, (rows, width), 1)
            damp = jnp.where(row_ids == col_ids, jnp.float32(damping), jnp.float32(0.0))
            for slab in range(4):
                here = slice(slab * lane, (slab + 1) * lane)
                mine, theirs = refs[i][0, :, here], refs[i][1, :, here]
                for other in range(2):
                    at = (2 * slab + other) * lane
                    there = pl.ds(pl.multiple_of(block * width + at, lane), lane)
                    out[:, there] = jnp.where(where[2] == other, mine, theirs) + damp[:, at : at + lane]

    return pl.pallas_call(
        kernel,
        grid_spec=pltpu.PrefetchScalarGridSpec(
            num_scalar_prefetch=1,
            grid=(1,),
            in_specs=[pl.BlockSpec(v.shape, lambda i, where: (0, 0, 0)) for v in sums]
            + [pl.BlockSpec(memory_space=pl.ANY)] * len(given),
            out_specs=pl.BlockSpec((rows, 4 * width), lambda i, where: (0, where[0])),
        ),
        out_shape=jax.ShapeDtypeStruct((rows, 8 * width), jnp.float32),
        input_output_aliases={5: 0} if given else {},
        compiler_params=pltpu.CompilerParams(vmem_limit_bytes=16 * mib),
    )(jnp.stack(where), *sums, *given)


def per_device(features):
    yh, x, z, yl, core = (lax.axis_index(name) for name in parts)
    rows, cols = features.shape
    half, part = cols // 2, cols // 16

    theirs, both = split(features, yl)
    near_mine = trade(theirs, ring, 1)
    both_away = swap(both)
    kept = turn(both, both_away, core)
    kept_near, kept_far = trade(kept, "x", 1), trade(kept, "x", 3)
    near_mine_away = swap(after(near_mine, kept_near, kept_far))
    got = turn(near_mine, near_mine_away, core)
    got_near, got_far = trade(got, "x", 1), trade(got, "x", 3)
    near_theirs = trade(after(both[0], near_mine), ring, 1)
    tick = swap(after(got[0, :8, :lane]))
    near_theirs_away = swap(near_theirs)
    got_near, got_far, near_theirs = together(got_near, got_far, near_theirs)
    kept_opposite, got_opposite = trade(after(kept_far, got_near), "x", 1), trade(got_near, "x", 3)
    lefts = [(kept, got), (kept_near, got_near), (kept_opposite, got_opposite), (kept_far, got_far)]
    far = trade(after(both, tick), ring, 3)

    first = [(both, 0), (both_away, 0), (near_mine, None), (near_mine_away, None)]
    first += [(both, 1), (both_away, 1), (near_theirs, None), (near_theirs_away, None)]
    tile = product([0, 1, 3], x, lefts, first)
    tile = product([2], x, lefts, first, result=tile)
    far, near_mine, tile = together(far, near_mine, tile)
    opposite_mine, opposite_theirs = trade(far[0], ring, 1), trade(near_mine, ring, 3)
    far_away = swap(far)
    second = [(opposite_mine, None), (swap(opposite_mine), None), (far, 1), (far_away, 1)]
    second += [(opposite_theirs, None), (swap(opposite_theirs), None), (far, 0), (far_away, 0)]

    first_row = ((((yh * 4 + x) * 4 + z) * 2 + yl) * 2 + core) * part
    zero = jnp.int32(0)
    result = None
    for side in range(2):
        if side:
            tile = product([0, 1, 2, 3], x, lefts, second)
        packed = tile.astype(jnp.float16).reshape(16, -1, 8, half)
        across = lax.all_to_all(packed, ("x", "z"), 0, 0, tiled=True)
        if side:
            across, result = together(across, result)
        sums = unscale(across.reshape(4, 4, -1, 8, half)).sum(1).reshape(4, 2, part, half)
        result = place([sums[i] for i in range(4)], [yh ^ side, first_row, yl] + [zero + i for i in range(4)], result)
    return result


def solution(mesh):
    fine = Mesh(mesh.devices.reshape(sizes), parts)
    return jax.shard_map(
        per_device,
        mesh=fine,
        in_specs=(P(("z", "yl", "core"), ("yh", "x")),),
        out_specs=P(parts, None),
        check_vma=False,
    )
```

```python
import jax
import jax.numpy as jnp
from jax import lax
from jax.experimental import pallas as pl
from jax.experimental.pallas import tpu as pltpu
from jax.sharding import Mesh, PartitionSpec as P

damping = 0.5
parts = ("yh", "x", "z", "yl", "core")
sizes = (2, 4, 4, 2, 2)
ring = ("yh", "yl")
mib = 1024 * 1024
lane = 128
top_power = 14.0


def swap(value):
    return lax.ppermute(value, "core", [(0, 1), (1, 0)])


def trade(value, axis, bits):
    return lax.ppermute(value, axis, [(i, i ^ bits) for i in range(4)])


def together(*values):
    return lax.optimization_barrier(values)


def in_hbm(value):
    return pltpu.with_memory_space_constraint(value, pltpu.HBM)


def after(value, *others):
    return lax.optimization_barrier((value, *others))[0]


vmem = pl.BlockSpec(memory_space=pltpu.VMEM)
smem = pl.BlockSpec(memory_space=pltpu.SMEM)


def split_kernel(place, block, theirs, both):
    yl = place[0]
    for slab in range(4):
        here = slice(slab * lane, (slab + 1) * lane)
        for other in range(2):
            start = pl.multiple_of((slab * 2 + (yl ^ other)) * lane, lane)
            some = block[:, pl.ds(start, lane)]
            both[other, :, here] = some
            if other:
                theirs[:, here] = some


def split(features, yl):
    rows, cols = features.shape
    return pl.pallas_call(
        split_kernel,
        in_specs=[smem, vmem],
        out_specs=[vmem] * 2,
        out_shape=[
            jax.ShapeDtypeStruct((rows, cols // 2), features.dtype),
            jax.ShapeDtypeStruct((2, rows, cols // 2), features.dtype),
        ],
        compiler_params=pltpu.CompilerParams(vmem_limit_bytes=16 * mib),
    )(jnp.stack([yl]), features)


def turn_kernel(place, *refs):
    core = place[0]
    *blocks, out = refs
    part = lane // 2
    for which, block in enumerate(blocks):
        for slab in range(4):
            here = slice(slab * lane, (slab + 1) * lane)
            turned = (block[0, :, here] if len(block.shape) == 3 else block[:, here]).T
            out[which, slab * part : (slab + 1) * part, :] = jnp.where(core == 0, turned[:part], turned[part:])


def turn(block, away, core):
    rows, cols = block.shape[-2:]
    first = pl.BlockSpec((1, rows, cols), lambda i: (0, 0, 0)) if block.ndim == 3 else pl.BlockSpec((rows, cols), lambda i: (0, 0))
    return pl.pallas_call(
        turn_kernel,
        grid=(1,),
        in_specs=[smem, first, first],
        out_specs=pl.BlockSpec((2, cols // 2, rows), lambda i: (0, 0, 0)),
        out_shape=jax.ShapeDtypeStruct((2, cols // 2, rows), block.dtype),
        compiler_params=pltpu.CompilerParams(vmem_limit_bytes=16 * mib),
    )(jnp.stack([core]), block, away)


def weights(cols):
    return 1.0 + lax.broadcasted_iota(jnp.int32, (1, cols), 1).astype(jnp.float32) / cols


def product(ns, turn_by, lefts, rights, by_z=False, result=None, alone=False):
    flat = [part for n in ns for part in lefts[n]]
    starts = [sum(len(lefts[m]) for m in ns[:i]) for i in range(len(ns))]
    arrays, picks = zip(*rights)
    rows, depth, cols, block = flat[0].shape[-2], flat[0].shape[-1], arrays[0].shape[-1], 512
    eights, one = rows // 4 // 8, result is not None

    def kernel(where, *refs):
        out = refs[-1]
        col = pl.program_id(0) * block + lax.broadcasted_iota(jnp.int32, (1, block), 1)
        weight = 1.0 + col.astype(jnp.float32) / cols
        for i, n in enumerate(ns):
            terms = []
            for ref in refs[starts[i] : starts[i] + len(lefts[n])]:
                terms += [ref[0], ref[1]] if len(ref.shape) == 3 else [ref[...]]
            totals, most = [], jnp.full((1, 1), 1e-30, jnp.float32)
            for c in range(2):
                total = None
                for t, left in enumerate(terms):
                    right = refs[len(flat) + 4 * c + t]
                    right = right[0] if len(right.shape) == 3 else right[...]
                    term = jnp.dot(left, right, preferred_element_type=jnp.float32)
                    total = term if total is None else total + term
                totals.append(total)
                most = jnp.maximum(most, jnp.max(jnp.max(jnp.abs(total), axis=0, keepdims=True), axis=1, keepdims=True))
            power = jnp.ceil(jnp.log2(most)) - top_power
            shrink = jnp.exp2(-power) * weight
            for slab in range(4):
                if by_z:
                    at = (slab ^ where[0], i)
                else:
                    at = (0 if one or alone else where[0] ^ n, slab)
                for c in range(2):
                    some = totals[c][slab * 8 * eights : (slab + 1) * 8 * eights] * shrink
                    out[(*at, slice(c * eights, (c + 1) * eights))] = some.reshape(eights, 8, block)
                out[(*at, 2 * eights)] = jnp.broadcast_to(power, (8, block))

    specs = [pl.BlockSpec(v.shape, lambda i, where, dims=v.ndim: (0,) * dims) for v in flat]
    for pick in picks:
        if pick is None:
            specs.append(pl.BlockSpec((depth, block), lambda i, where: (0, i)))
        else:
            specs.append(pl.BlockSpec((1, depth, block), lambda i, where, pick=pick: (pick, 0, i)))
    height = 2 * eights + 1
    if one:
        specs.append(pl.BlockSpec(memory_space=pl.ANY))
    count, slots = (len(ns) if by_z else 4), (1 if alone else 4)
    if one:
        out_spec = pl.BlockSpec((1, 4, height, 8, block), lambda i, where: (where[0] ^ ns[0], 0, 0, 0, i))
    else:
        out_spec = pl.BlockSpec((slots, count, height, 8, block), lambda i, where: (0, 0, 0, 0, i))
    return pl.pallas_call(
        kernel,
        grid_spec=pltpu.PrefetchScalarGridSpec(
            num_scalar_prefetch=1, grid=(cols // block,), in_specs=specs, out_specs=out_spec
        ),
        out_shape=jax.ShapeDtypeStruct((slots, count, height, 8, cols), jnp.float32),
        input_output_aliases={len(specs): 0} if one else {},
        compiler_params=pltpu.CompilerParams(vmem_limit_bytes=32 * mib),
        cost_estimate=pl.CostEstimate(
            flops=2 * rows * cols * depth * len(arrays) * len(ns), bytes_accessed=8 * mib, transcendentals=0
        ),
    )(jnp.stack([turn_by]), *[in_hbm(v) if n in (1, 3) else v for n in ns for v in lefts[n]], *arrays, *([result] if one else []))


def unscale(value):
    grow = jnp.exp2(value[..., -1:, :, :].astype(jnp.float32)) / weights(value.shape[-1])
    return value[..., :-1, :, :].astype(jnp.float32) * grow


def place(sums, where, result=None):
    _, rows, half = sums[0].shape
    width = 2 * half
    given = [] if result is None else [result]

    def kernel(where, *refs):
        out = refs[-1]
        for i in range(4):
            block = where[3 + i]
            row_ids = where[1] + lax.broadcasted_iota(jnp.int32, (rows, width), 0)
            col_ids = (where[0] * 4 + block) * width + lax.broadcasted_iota(jnp.int32, (rows, width), 1)
            damp = jnp.where(row_ids == col_ids, jnp.float32(damping), jnp.float32(0.0))
            for slab in range(4):
                here = slice(slab * lane, (slab + 1) * lane)
                mine, theirs = refs[i][0, :, here], refs[i][1, :, here]
                for other in range(2):
                    at = (2 * slab + other) * lane
                    there = pl.ds(pl.multiple_of(block * width + at, lane), lane)
                    out[:, there] = jnp.where(where[2] == other, mine, theirs) + damp[:, at : at + lane]

    return pl.pallas_call(
        kernel,
        grid_spec=pltpu.PrefetchScalarGridSpec(
            num_scalar_prefetch=1,
            grid=(1,),
            in_specs=[pl.BlockSpec(v.shape, lambda i, where: (0, 0, 0)) for v in sums]
            + [pl.BlockSpec(memory_space=pl.ANY)] * len(given),
            out_specs=pl.BlockSpec((rows, 4 * width), lambda i, where: (0, where[0])),
        ),
        out_shape=jax.ShapeDtypeStruct((rows, 8 * width), jnp.float32),
        input_output_aliases={5: 0} if given else {},
        compiler_params=pltpu.CompilerParams(vmem_limit_bytes=16 * mib),
    )(jnp.stack(where), *sums, *given)


def per_device(features):
    yh, x, z, yl, core = (lax.axis_index(name) for name in parts)
    rows, cols = features.shape
    half, part = cols // 2, cols // 16

    theirs, both = split(features, yl)
    near_mine = trade(theirs, ring, 1)
    both_away = swap(both)
    kept = turn(both, both_away, core)
    kept_near, kept_far = trade(kept, "x", 1), trade(kept, "x", 3)
    near_mine_away = swap(after(near_mine, kept_near, kept_far))
    got = turn(near_mine, near_mine_away, core)
    got_near, got_far = trade(got, "x", 1), trade(got, "x", 3)
    near_theirs = trade(after(both[0], near_mine), ring, 1)
    tick = swap(after(got[0, :8, :lane]))
    near_theirs_away = swap(near_theirs)
    got_near, got_far, near_theirs = together(got_near, got_far, near_theirs)
    kept_opposite, got_opposite = trade(after(kept_far, got_near), "x", 1), trade(got_near, "x", 3)
    lefts = [(kept, got), (kept_near, got_near), (kept_opposite, got_opposite), (kept_far, got_far)]
    far = trade(after(both, tick), ring, 3)

    first = [(both, 0), (both_away, 0), (near_mine, None), (near_mine_away, None)]
    first += [(both, 1), (both_away, 1), (near_theirs, None), (near_theirs_away, None)]
    tile = product([0, 1, 3], x, lefts, first)
    tile = tile.astype(jnp.float16)
    last = product([2], x, lefts, first, alone=True).astype(jnp.float16)
    tile = lax.dynamic_update_slice_in_dim(tile, last, x ^ 2, 0)
    far, near_mine, _ = together(far, near_mine, tile)
    opposite_mine, opposite_theirs = trade(far[0], ring, 1), trade(near_mine, ring, 3)
    far_away = swap(far)
    second = [(opposite_mine, None), (swap(opposite_mine), None), (far, 1), (far_away, 1)]
    second += [(opposite_theirs, None), (swap(opposite_theirs), None), (far, 0), (far_away, 0)]

    first_row = ((((yh * 4 + x) * 4 + z) * 2 + yl) * 2 + core) * part
    zero = jnp.int32(0)
    result = None
    for side in range(2):
        if side:
            tile = product([0, 1, 2, 3], x, lefts, second)
        packed = tile.astype(jnp.float16).reshape(16, -1, 8, half)
        across = lax.all_to_all(packed, ("x", "z"), 0, 0, tiled=True)
        if side:
            across, result = together(across, result)
        sums = unscale(across.reshape(4, 4, -1, 8, half)).sum(1).reshape(4, 2, part, half)
        result = place([sums[i] for i in range(4)], [yh ^ side, first_row, yl] + [zero + i for i in range(4)], result)
    return result


def solution(mesh):
    fine = Mesh(mesh.devices.reshape(sizes), parts)
    return jax.shard_map(
        per_device,
        mesh=fine,
        in_specs=(P(("z", "yl", "core"), ("yh", "x")),),
        out_specs=P(parts, None),
        check_vma=False,
    )
```

```python
import jax
import jax.numpy as jnp
from jax import lax
from jax.experimental import pallas as pl
from jax.experimental.pallas import tpu as pltpu
from jax.sharding import Mesh, PartitionSpec as P

damping = 0.5
parts = ("yh", "x", "z", "yl", "core")
sizes = (2, 4, 4, 2, 2)
ring = ("yh", "yl")
mib = 1024 * 1024
lane = 128
top_power = 14.0


def swap(value):
    return lax.ppermute(value, "core", [(0, 1), (1, 0)])


def trade(value, axis, bits):
    return lax.ppermute(value, axis, [(i, i ^ bits) for i in range(4)])


def together(*values):
    return lax.optimization_barrier(values)


def in_hbm(value):
    return pltpu.with_memory_space_constraint(value, pltpu.HBM)


def after(value, *others):
    return lax.optimization_barrier((value, *others))[0]


vmem = pl.BlockSpec(memory_space=pltpu.VMEM)
smem = pl.BlockSpec(memory_space=pltpu.SMEM)


def split_kernel(place, block, theirs, both):
    yl = place[0]
    for slab in range(4):
        here = slice(slab * lane, (slab + 1) * lane)
        for other in range(2):
            start = pl.multiple_of((slab * 2 + (yl ^ other)) * lane, lane)
            some = block[:, pl.ds(start, lane)]
            both[other, :, here] = some
            if other:
                theirs[:, here] = some


def split(features, yl):
    rows, cols = features.shape
    return pl.pallas_call(
        split_kernel,
        in_specs=[smem, vmem],
        out_specs=[vmem] * 2,
        out_shape=[
            jax.ShapeDtypeStruct((rows, cols // 2), features.dtype),
            jax.ShapeDtypeStruct((2, rows, cols // 2), features.dtype),
        ],
        compiler_params=pltpu.CompilerParams(vmem_limit_bytes=16 * mib),
    )(jnp.stack([yl]), features)


def turn_kernel(place, *refs):
    core = place[0]
    *blocks, out = refs
    part = lane // 2
    for which, block in enumerate(blocks):
        for slab in range(4):
            here = slice(slab * lane, (slab + 1) * lane)
            turned = (block[0, :, here] if len(block.shape) == 3 else block[:, here]).T
            out[which, slab * part : (slab + 1) * part, :] = jnp.where(core == 0, turned[:part], turned[part:])


def turn(block, away, core):
    rows, cols = block.shape[-2:]
    first = pl.BlockSpec((1, rows, cols), lambda i: (0, 0, 0)) if block.ndim == 3 else pl.BlockSpec((rows, cols), lambda i: (0, 0))
    return pl.pallas_call(
        turn_kernel,
        grid=(1,),
        in_specs=[smem, first, first],
        out_specs=pl.BlockSpec((2, cols // 2, rows), lambda i: (0, 0, 0)),
        out_shape=jax.ShapeDtypeStruct((2, cols // 2, rows), block.dtype),
        compiler_params=pltpu.CompilerParams(vmem_limit_bytes=16 * mib),
    )(jnp.stack([core]), block, away)


def weights(cols):
    return 1.0 + lax.broadcasted_iota(jnp.int32, (1, cols), 1).astype(jnp.float32) / cols


def product(ns, turn_by, lefts, rights, by_z=False, result=None, alone=False):
    flat = [part for n in ns for part in lefts[n]]
    starts = [sum(len(lefts[m]) for m in ns[:i]) for i in range(len(ns))]
    arrays, picks = zip(*rights)
    rows, depth, cols, block = flat[0].shape[-2], flat[0].shape[-1], arrays[0].shape[-1], 512
    eights, one = rows // 4 // 8, result is not None

    def kernel(where, *refs):
        out = refs[-1]
        col = pl.program_id(0) * block + lax.broadcasted_iota(jnp.int32, (1, block), 1)
        weight = 1.0 + col.astype(jnp.float32) / cols
        for i, n in enumerate(ns):
            terms = []
            for ref in refs[starts[i] : starts[i] + len(lefts[n])]:
                terms += [ref[0], ref[1]] if len(ref.shape) == 3 else [ref[...]]
            totals, most = [], jnp.full((1, 1), 1e-30, jnp.float32)
            for c in range(2):
                total = None
                for t, left in enumerate(terms):
                    right = refs[len(flat) + 4 * c + t]
                    right = right[0] if len(right.shape) == 3 else right[...]
                    term = jnp.dot(left, right, preferred_element_type=jnp.float32)
                    total = term if total is None else total + term
                totals.append(total)
                most = jnp.maximum(most, jnp.max(jnp.max(jnp.abs(total), axis=0, keepdims=True), axis=1, keepdims=True))
            power = jnp.ceil(jnp.log2(most)) - top_power
            shrink = jnp.exp2(-power) * weight
            for slab in range(4):
                if by_z:
                    at = (slab ^ where[0], i)
                else:
                    at = (0 if one or alone else where[0] ^ n, slab)
                for c in range(2):
                    some = totals[c][slab * 8 * eights : (slab + 1) * 8 * eights] * shrink
                    out[(*at, slice(c * eights, (c + 1) * eights))] = some.reshape(eights, 8, block)
                out[(*at, 2 * eights)] = jnp.broadcast_to(power, (8, block))

    specs = [pl.BlockSpec(v.shape, lambda i, where, dims=v.ndim: (0,) * dims) for v in flat]
    for pick in picks:
        if pick is None:
            specs.append(pl.BlockSpec((depth, block), lambda i, where: (0, i)))
        else:
            specs.append(pl.BlockSpec((1, depth, block), lambda i, where, pick=pick: (pick, 0, i)))
    height = 2 * eights + 1
    if one:
        specs.append(pl.BlockSpec(memory_space=pl.ANY))
    count, slots = (len(ns) if by_z else 4), (1 if alone else 4)
    if one:
        out_spec = pl.BlockSpec((1, 4, height, 8, block), lambda i, where: (where[0] ^ ns[0], 0, 0, 0, i))
    else:
        out_spec = pl.BlockSpec((slots, count, height, 8, block), lambda i, where: (0, 0, 0, 0, i))
    return pl.pallas_call(
        kernel,
        grid_spec=pltpu.PrefetchScalarGridSpec(
            num_scalar_prefetch=1, grid=(cols // block,), in_specs=specs, out_specs=out_spec
        ),
        out_shape=jax.ShapeDtypeStruct((slots, count, height, 8, cols), jnp.float32),
        input_output_aliases={len(specs): 0} if one else {},
        compiler_params=pltpu.CompilerParams(vmem_limit_bytes=32 * mib),
        cost_estimate=pl.CostEstimate(
            flops=2 * rows * cols * depth * len(arrays) * len(ns), bytes_accessed=8 * mib, transcendentals=0
        ),
    )(jnp.stack([turn_by]), *[in_hbm(v) if n in (1, 3) else v for n in ns for v in lefts[n]], *arrays, *([result] if one else []))


def unscale(value):
    grow = jnp.exp2(value[..., -1:, :, :].astype(jnp.float32)) / weights(value.shape[-1])
    return value[..., :-1, :, :].astype(jnp.float32) * grow


def place(sums, where, result=None):
    own = result is None
    _, rows, half = sums[0].shape
    width = 2 * half
    given = [] if result is None else [result]

    def kernel(where, *refs):
        out = refs[-1]
        for i in range(4):
            block = where[3 + i]
            if own:
                row_ids = where[1] + lax.broadcasted_iota(jnp.int32, (rows, width), 0)
                col_ids = (where[0] * 4 + block) * width + lax.broadcasted_iota(jnp.int32, (rows, width), 1)
                damp = jnp.where(row_ids == col_ids, jnp.float32(damping), jnp.float32(0.0))
            for slab in range(4):
                here = slice(slab * lane, (slab + 1) * lane)
                mine, theirs = refs[i][0, :, here], refs[i][1, :, here]
                for other in range(2):
                    at = (2 * slab + other) * lane
                    there = pl.ds(pl.multiple_of(block * width + at, lane), lane)
                    value = jnp.where(where[2] == other, mine, theirs)
                    out[:, there] = value + damp[:, at : at + lane] if own else value

    return pl.pallas_call(
        kernel,
        grid_spec=pltpu.PrefetchScalarGridSpec(
            num_scalar_prefetch=1,
            grid=(1,),
            in_specs=[vmem] * len(sums)
            + [pl.BlockSpec(memory_space=pl.ANY)] * len(given),
            out_specs=pl.BlockSpec((rows, 4 * width), lambda i, where: (0, where[0])),
        ),
        out_shape=jax.ShapeDtypeStruct((rows, 8 * width), jnp.float32),
        input_output_aliases={5: 0} if given else {},
        compiler_params=pltpu.CompilerParams(vmem_limit_bytes=16 * mib),
    )(jnp.stack(where), *sums, *given)


def per_device(features):
    yh, x, z, yl, core = (lax.axis_index(name) for name in parts)
    rows, cols = features.shape
    half, part = cols // 2, cols // 16

    theirs, both = split(features, yl)
    near_mine = trade(theirs, ring, 1)
    both_away = swap(both)
    kept = turn(both, both_away, core)
    kept_near, kept_far = trade(kept, "x", 1), trade(kept, "x", 3)
    near_mine_away = swap(after(near_mine, kept_near, kept_far))
    got = turn(near_mine, near_mine_away, core)
    got_near, got_far = trade(got, "x", 1), trade(got, "x", 3)
    near_theirs = trade(after(both[0], near_mine), ring, 1)
    tick = swap(after(got[0, :8, :lane]))
    near_theirs_away = swap(near_theirs)
    got_near, got_far, near_theirs = together(got_near, got_far, near_theirs)
    kept_opposite, got_opposite = trade(after(kept_far, got_near), "x", 1), trade(got_near, "x", 3)
    lefts = [(kept, got), (kept_near, got_near), (kept_opposite, got_opposite), (kept_far, got_far)]
    far = trade(after(both, tick), ring, 3)

    first = [(both, 0), (both_away, 0), (near_mine, None), (near_mine_away, None)]
    first += [(both, 1), (both_away, 1), (near_theirs, None), (near_theirs_away, None)]
    tile = product([0, 1, 3], x, lefts, first)
    tile = tile.astype(jnp.float16)
    last = product([2], x, lefts, first, alone=True).astype(jnp.float16)
    tile = lax.dynamic_update_slice_in_dim(tile, last, x ^ 2, 0)
    far, near_mine, _ = together(far, near_mine, tile)
    opposite_mine, opposite_theirs = trade(far[0], ring, 1), trade(near_mine, ring, 3)
    far_away = swap(far)
    second = [(opposite_mine, None), (swap(opposite_mine), None), (far, 1), (far_away, 1)]
    second += [(opposite_theirs, None), (swap(opposite_theirs), None), (far, 0), (far_away, 0)]

    first_row = ((((yh * 4 + x) * 4 + z) * 2 + yl) * 2 + core) * part
    zero = jnp.int32(0)
    result = None
    for side in range(2):
        if side:
            tile = product([0, 1, 2, 3], x, lefts, second)
        packed = tile.astype(jnp.float16).reshape(16, -1, 8, half)
        across = lax.all_to_all(packed, ("x", "z"), 0, 0, tiled=True)
        if side:
            across, result = together(across, result)
        sums = unscale(across.reshape(4, 4, -1, 8, half)).sum(1).reshape(4, 2, part, half)
        result = place([sums[i] for i in range(4)], [yh ^ side, first_row, yl] + [zero + i for i in range(4)], result)
    return result


def solution(mesh):
    fine = Mesh(mesh.devices.reshape(sizes), parts)
    return jax.shard_map(
        per_device,
        mesh=fine,
        in_specs=(P(("z", "yl", "core"), ("yh", "x")),),
        out_specs=P(parts, None),
        check_vma=False,
    )
```

```python
import jax
import jax.numpy as jnp
from jax import lax
from jax.experimental import pallas as pl
from jax.experimental.pallas import tpu as pltpu
from jax.sharding import Mesh, PartitionSpec as P

damping = 0.5
parts = ("yh", "x", "z", "yl", "core")
sizes = (2, 4, 4, 2, 2)
ring = ("yh", "yl")
mib = 1024 * 1024
lane = 128
top_power = 14.0


def swap(value):
    return lax.ppermute(value, "core", [(0, 1), (1, 0)])


def trade(value, axis, bits):
    return lax.ppermute(value, axis, [(i, i ^ bits) for i in range(4)])


def together(*values):
    return lax.optimization_barrier(values)


def in_hbm(value):
    return pltpu.with_memory_space_constraint(value, pltpu.HBM)


def after(value, *others):
    return lax.optimization_barrier((value, *others))[0]


vmem = pl.BlockSpec(memory_space=pltpu.VMEM)
smem = pl.BlockSpec(memory_space=pltpu.SMEM)


def split_kernel(place, block, theirs, both):
    yl = place[0]
    for slab in range(4):
        here = slice(slab * lane, (slab + 1) * lane)
        for other in range(2):
            start = pl.multiple_of((slab * 2 + (yl ^ other)) * lane, lane)
            some = block[:, pl.ds(start, lane)]
            both[other, :, here] = some
            if other:
                theirs[:, here] = some


def split(features, yl):
    rows, cols = features.shape
    return pl.pallas_call(
        split_kernel,
        in_specs=[smem, vmem],
        out_specs=[vmem] * 2,
        out_shape=[
            jax.ShapeDtypeStruct((rows, cols // 2), features.dtype),
            jax.ShapeDtypeStruct((2, rows, cols // 2), features.dtype),
        ],
        compiler_params=pltpu.CompilerParams(vmem_limit_bytes=16 * mib),
    )(jnp.stack([yl]), features)


def turn_kernel(place, *refs):
    core = place[0]
    *blocks, out = refs
    part = lane // 2
    for which, block in enumerate(blocks):
        for slab in range(4):
            here = slice(slab * lane, (slab + 1) * lane)
            turned = (block[0, :, here] if len(block.shape) == 3 else block[:, here]).T
            out[which, slab * part : (slab + 1) * part, :] = jnp.where(core == 0, turned[:part], turned[part:])


def turn(block, away, core):
    rows, cols = block.shape[-2:]
    first = pl.BlockSpec((1, rows, cols), lambda i: (0, 0, 0)) if block.ndim == 3 else pl.BlockSpec((rows, cols), lambda i: (0, 0))
    return pl.pallas_call(
        turn_kernel,
        grid=(1,),
        in_specs=[smem, first, first],
        out_specs=pl.BlockSpec((2, cols // 2, rows), lambda i: (0, 0, 0)),
        out_shape=jax.ShapeDtypeStruct((2, cols // 2, rows), block.dtype),
        compiler_params=pltpu.CompilerParams(vmem_limit_bytes=16 * mib),
    )(jnp.stack([core]), block, away)


def weights(cols):
    return 1.0 + lax.broadcasted_iota(jnp.int32, (1, cols), 1).astype(jnp.float32) / cols


def product(ns, turn_by, lefts, rights, by_z=False, result=None, alone=False):
    flat = [part for n in ns for part in lefts[n]]
    starts = [sum(len(lefts[m]) for m in ns[:i]) for i in range(len(ns))]
    arrays, picks = zip(*rights)
    rows, depth, cols, block = flat[0].shape[-2], flat[0].shape[-1], arrays[0].shape[-1], 512
    eights, one = rows // 4 // 8, result is not None

    def kernel(where, *refs):
        out = refs[-1]
        col = pl.program_id(0) * block + lax.broadcasted_iota(jnp.int32, (1, block), 1)
        weight = 1.0 + col.astype(jnp.float32) / cols
        for i, n in enumerate(ns):
            terms = []
            for ref in refs[starts[i] : starts[i] + len(lefts[n])]:
                terms += [ref[0], ref[1]] if len(ref.shape) == 3 else [ref[...]]
            totals, most = [], jnp.full((1, 1), 1e-30, jnp.float32)
            for c in range(2):
                total = None
                for t, left in enumerate(terms):
                    right = refs[len(flat) + 4 * c + t]
                    right = right[0] if len(right.shape) == 3 else right[...]
                    term = jnp.dot(left, right, preferred_element_type=jnp.float32)
                    total = term if total is None else total + term
                totals.append(total)
                most = jnp.maximum(most, jnp.max(jnp.max(jnp.abs(total), axis=0, keepdims=True), axis=1, keepdims=True))
            power = jnp.ceil(jnp.log2(most)) - top_power
            shrink = jnp.exp2(-power) * weight
            for slab in range(4):
                if by_z:
                    at = (slab ^ where[0], i)
                else:
                    at = (0 if one or alone else where[0] ^ n, slab)
                for c in range(2):
                    some = totals[c][slab * 8 * eights : (slab + 1) * 8 * eights] * shrink
                    out[(*at, slice(c * eights, (c + 1) * eights))] = some.reshape(eights, 8, block)
                out[(*at, 2 * eights)] = jnp.broadcast_to(power, (8, block))

    specs = [pl.BlockSpec(v.shape, lambda i, where, dims=v.ndim: (0,) * dims) for v in flat]
    for pick in picks:
        if pick is None:
            specs.append(pl.BlockSpec((depth, block), lambda i, where: (0, i)))
        else:
            specs.append(pl.BlockSpec((1, depth, block), lambda i, where, pick=pick: (pick, 0, i)))
    height = 2 * eights + 1
    if one:
        specs.append(pl.BlockSpec(memory_space=pl.ANY))
    count, slots = (len(ns) if by_z else 4), (1 if alone else 4)
    if one:
        out_spec = pl.BlockSpec((1, 4, height, 8, block), lambda i, where: (where[0] ^ ns[0], 0, 0, 0, i))
    else:
        out_spec = pl.BlockSpec((slots, count, height, 8, block), lambda i, where: (0, 0, 0, 0, i))
    return pl.pallas_call(
        kernel,
        grid_spec=pltpu.PrefetchScalarGridSpec(
            num_scalar_prefetch=1, grid=(cols // block,), in_specs=specs, out_specs=out_spec
        ),
        out_shape=jax.ShapeDtypeStruct((slots, count, height, 8, cols), jnp.float32),
        input_output_aliases={len(specs): 0} if one else {},
        compiler_params=pltpu.CompilerParams(vmem_limit_bytes=32 * mib),
        cost_estimate=pl.CostEstimate(
            flops=2 * rows * cols * depth * len(arrays) * len(ns), bytes_accessed=8 * mib, transcendentals=0
        ),
    )(jnp.stack([turn_by]), *flat, *arrays, *([result] if one else []))


def unscale(value):
    grow = jnp.exp2(value[..., -1:, :, :].astype(jnp.float32)) / weights(value.shape[-1])
    return value[..., :-1, :, :].astype(jnp.float32) * grow


def place(sums, where, result=None):
    own = result is None
    _, rows, half = sums[0].shape
    width = 2 * half
    given = [] if result is None else [result]

    def kernel(where, *refs):
        out = refs[-1]
        for i in range(4):
            block = where[3 + i]
            if own:
                row_ids = where[1] + lax.broadcasted_iota(jnp.int32, (rows, width), 0)
                col_ids = (where[0] * 4 + block) * width + lax.broadcasted_iota(jnp.int32, (rows, width), 1)
                damp = jnp.where(row_ids == col_ids, jnp.float32(damping), jnp.float32(0.0))
            for slab in range(4):
                here = slice(slab * lane, (slab + 1) * lane)
                mine, theirs = refs[i][0, :, here], refs[i][1, :, here]
                for other in range(2):
                    at = (2 * slab + other) * lane
                    there = pl.ds(pl.multiple_of(block * width + at, lane), lane)
                    value = jnp.where(where[2] == other, mine, theirs)
                    out[:, there] = value + damp[:, at : at + lane] if own else value

    return pl.pallas_call(
        kernel,
        grid_spec=pltpu.PrefetchScalarGridSpec(
            num_scalar_prefetch=1,
            grid=(1,),
            in_specs=[vmem] * len(sums)
            + [pl.BlockSpec(memory_space=pl.ANY)] * len(given),
            out_specs=pl.BlockSpec((rows, 4 * width), lambda i, where: (0, where[0])),
        ),
        out_shape=jax.ShapeDtypeStruct((rows, 8 * width), jnp.float32),
        input_output_aliases={5: 0} if given else {},
        compiler_params=pltpu.CompilerParams(vmem_limit_bytes=16 * mib),
    )(jnp.stack(where), *sums, *given)


def per_device(features):
    yh, x, z, yl, core = (lax.axis_index(name) for name in parts)
    rows, cols = features.shape
    half, part = cols // 2, cols // 16

    theirs, both = split(features, yl)
    near_mine = trade(theirs, ring, 1)
    both_away = swap(both)
    kept = turn(both, both_away, core)
    kept_near, kept_far = in_hbm(trade(kept, "x", 1)), in_hbm(trade(kept, "x", 3))
    near_mine_away = swap(after(near_mine, kept_near, kept_far))
    got = turn(near_mine, near_mine_away, core)
    got_near, got_far = in_hbm(trade(got, "x", 1)), in_hbm(trade(got, "x", 3))
    near_theirs = trade(after(both[0], near_mine), ring, 1)
    tick = swap(after(got[0, :8, :lane]))
    near_theirs_away = swap(near_theirs)
    got_near, got_far, near_theirs = together(got_near, got_far, near_theirs)
    kept_opposite, got_opposite = trade(after(kept_far, got_near), "x", 1), trade(got_near, "x", 3)
    lefts = [(kept, got), (kept_near, got_near), (kept_opposite, got_opposite), (kept_far, got_far)]
    far = trade(after(both, tick), ring, 3)

    first = [(both, 0), (both_away, 0), (near_mine, None), (near_mine_away, None)]
    first += [(both, 1), (both_away, 1), (near_theirs, None), (near_theirs_away, None)]
    tile = product([0, 1, 3], x, lefts, first)
    tile = tile.astype(jnp.float16)
    last = product([2], x, lefts, first, alone=True).astype(jnp.float16)
    tile = lax.dynamic_update_slice_in_dim(tile, last, x ^ 2, 0)
    far, near_mine, _ = together(far, near_mine, tile)
    opposite_mine, opposite_theirs = trade(far[0], ring, 1), trade(near_mine, ring, 3)
    far_away = swap(far)
    second = [(opposite_mine, None), (swap(opposite_mine), None), (far, 1), (far_away, 1)]
    second += [(opposite_theirs, None), (swap(opposite_theirs), None), (far, 0), (far_away, 0)]

    first_row = ((((yh * 4 + x) * 4 + z) * 2 + yl) * 2 + core) * part
    zero = jnp.int32(0)
    result = None
    for side in range(2):
        if side:
            tile = product([0, 1, 2, 3], x, lefts, second)
        packed = tile.astype(jnp.float16).reshape(16, -1, 8, half)
        across = lax.all_to_all(packed, ("x", "z"), 0, 0, tiled=True)
        if side:
            across, result = together(across, result)
        sums = unscale(across.reshape(4, 4, -1, 8, half)).sum(1).reshape(4, 2, part, half)
        result = place([sums[i] for i in range(4)], [yh ^ side, first_row, yl] + [zero + i for i in range(4)], result)
    return result


def solution(mesh):
    fine = Mesh(mesh.devices.reshape(sizes), parts)
    return jax.shard_map(
        per_device,
        mesh=fine,
        in_specs=(P(("z", "yl", "core"), ("yh", "x")),),
        out_specs=P(parts, None),
        check_vma=False,
    )
```
